32 devices in a mesh: gx: 16 (over z, y, core), gz: 2 (over x).
Axes of the slice: x: 2, y: 2, z: 4, core: 2. Of those that a mesh axis runs over, the one named last changes fastest.
Arguments:
- adjoint: bfloat16 [3, 128, 64, 256], P(None, 'gx', 'gz'), may hold values from -6 to 6
- strain: bfloat16 [128, 64, 256], P('gx', 'gz'), may hold values from -6 to 6
- correction: float32 [64, 256], P('gz'), may hold values from 0.3 to 3
- metric: float32 [256], replicated, may hold values from 0.5 to 4
- stream_inverse: bfloat16 [128, 128], replicated, may hold values from -0.081 to 1.081
- span_inverse: bfloat16 [64, 64], replicated, may hold values from -0.081 to 1.081
- wall_operator: bfloat16 [256, 256], replicated, may hold values from -0.081 to 1.081
Outputs:
- adjoint_next: bfloat16 [3, 128, 64, 256], P(None, 'gx', 'gz')
- gradient: float32 [64, 256], P('gz', 'gx')
The draws below stay inside these ranges and needn't reach their ends.
All inputs are finite; a program needn't handle non-finite values.
Results may differ from the reference program's by a relative error of at most 0.013.
Values may be sent and summed in bfloat16 or wider, within the bound.
A program may use at most 64 MiB of HBM per device.

```python
import math
import jax
import jax.numpy as jnp
from jax import lax

NY = 256
NX = 128
NZ = 64


def inverse_block(key, order):
    spread = jax.random.uniform(key, (order, order), jnp.float32, -0.08, 0.08)
    return spread + jnp.eye(order, dtype=jnp.float32)


def draw_stream_inverse(key, part):
    return inverse_block(jax.random.fold_in(key, 11), NX).astype(jnp.bfloat16)


def draw_span_inverse(key, part):
    return inverse_block(jax.random.fold_in(key, 23), NZ).astype(jnp.bfloat16)


def draw_wall_operator(key, part):
    return inverse_block(jax.random.fold_in(key, 37), NY).astype(jnp.bfloat16)


def strengthened(values, own_key, source, target, blocks, factor):
    owner, partner = [(jnp.arange(values.shape[position]) // (values.shape[position] // blocks)).reshape([-1 if axis == position else 1 for axis in range(values.ndim)]) for position in (source, target)]
    chosen = jax.random.permutation(own_key, blocks)[partner]
    strong = (owner == chosen) | (owner == (partner + blocks // 2) % blocks)
    return jnp.where(strong, factor * values, values)


def level_of(own_key, shape, shards, smallest, top_value):
    factor_of, own = 1.0, jax.random.fold_in(own_key, 6)
    for position, blocks in shards:
        steps = jnp.exp(jax.random.uniform(jax.random.fold_in(own, position), (blocks,), jnp.float32, smallest / len(shards), top_value / len(shards)))
        factor_of = factor_of * jnp.repeat(steps, shape[position] // blocks).reshape([-1 if axis == position else 1 for axis in range(len(shape))])
    return factor_of


def noise(rng, shape, scale, most, cuts=(), kind=jnp.bfloat16):
    loudness = level_of(rng, shape, cuts, -0.22, 0.18) if cuts else 1.0
    drawn = jax.random.normal(rng, shape, jnp.float32) * scale * loudness
    return jnp.minimum(jnp.maximum(drawn, -most), most).astype(kind)


def bell_draw_with(own_key, shape, deviation, reach, split, heavy, kind=jnp.bfloat16):
    array = deviation * jax.random.normal(own_key, shape, jnp.float32)
    if split:
        array = array * level_of(own_key, shape, split, -0.22, 0.18)
    return jnp.clip(strengthened(array, jax.random.fold_in(own_key, 3), *heavy), -reach, reach).astype(kind)


def setup_inputs(seed: int = 0) -> dict:
    streams_of = jax.random.split(jax.random.key(seed), 8)
    return {
        "adjoint": noise(streams_of[0], (3, NX, NZ, NY), 1.0, 6.0, ((1, 16), (2, 2))),
        "strain": bell_draw_with(streams_of[1], (NX, NZ, NY), 1.0, 6.0, ((0, 16), (1, 2)), (0, 2, 16, 2.0)),
        "correction": jnp.clip(jnp.exp(math.log(3.0) - 2.3025851 * jax.random.uniform(streams_of[2], (NZ, NY), jnp.float32) ** level_of(streams_of[2], (NZ, NY), ((0, 2),), -0.2, 0.2)), 0.3, 3.0),
        "metric": jnp.clip(jnp.exp(jax.random.uniform(streams_of[3], (NY,), jnp.float32, math.log(0.5), math.log(4.0))), 0.5, 4.0),
        "stream_inverse": draw_stream_inverse(jax.random.fold_in(streams_of[7], 71), 0),
        "span_inverse": draw_span_inverse(jax.random.fold_in(streams_of[7], 71), 0),
        "wall_operator": draw_wall_operator(jax.random.fold_in(streams_of[7], 71), 0),
    }


near_coef = 7.0 / 9.0
far_coef = 1.0 / 36.0
time_step = 0.25


def stencil(source, axis):
    widened = source.astype(jnp.float32)
    near_diff = jnp.roll(widened, -1, axis) - jnp.roll(widened, 1, axis)
    far_diff = jnp.roll(widened, -2, axis) - jnp.roll(widened, 2, axis)
    return (near_coef * near_diff + far_coef * far_diff).astype(jnp.bfloat16)


def reference(adjoint, strain, correction, metric, stream_inverse, span_inverse, wall_operator):
    strain_wide = strain.astype(jnp.float32)
    viscosity = (correction[None] * strain_wide).astype(jnp.bfloat16)
    viscous = viscosity.astype(jnp.float32)
    stream_wide = stream_inverse.astype(jnp.float32)
    span_wide = span_inverse.astype(jnp.float32)
    wall_wide = wall_operator.astype(jnp.float32)

    def stream_derivative(source):
        right_side = stencil(source, 0).astype(jnp.float32)
        return jnp.einsum('ij,jzy->izy', stream_wide, right_side).astype(jnp.bfloat16)

    def span_derivative(source):
        right_side = stencil(source, 1).astype(jnp.float32)
        return jnp.einsum('ij,xjy->xiy', span_wide, right_side).astype(jnp.bfloat16)

    def wall_derivative(source):
        return jnp.einsum('xzj,ij->xzi', source.astype(jnp.float32), wall_wide) * metric

    def per_component(source):
        stream_grad = stream_derivative(source)
        wall_grad = wall_derivative(source).astype(jnp.bfloat16)
        span_grad = span_derivative(source)
        stream_flux = (viscous * stream_grad.astype(jnp.float32)).astype(jnp.bfloat16)
        wall_flux = (viscous * wall_grad.astype(jnp.float32)).astype(jnp.bfloat16)
        span_flux = (viscous * span_grad.astype(jnp.float32)).astype(jnp.bfloat16)
        total = stream_derivative(stream_flux).astype(jnp.float32) + wall_derivative(wall_flux)
        total = total + span_derivative(span_flux).astype(jnp.float32)
        updated = (source.astype(jnp.float32) + time_step * total).astype(jnp.bfloat16)
        squares = stream_grad.astype(jnp.float32) ** 2 + wall_grad.astype(jnp.float32) ** 2
        squares = squares + span_grad.astype(jnp.float32) ** 2
        return updated, jnp.sum(strain_wide * squares, axis=0)

    new_fields, dissipation = lax.map(per_component, adjoint)
    gradient = -jnp.sum(dissipation, axis=0) / NX
    return new_fields, gradient
```

```python
import functools

import jax
import jax.numpy as jnp
from jax import lax
from jax.experimental import pallas as pl
from jax.experimental.pallas import tpu as pltpu
from jax.sharding import PartitionSpec as P

near_coef = 7.0 / 9.0
far_coef = 1.0 / 36.0
time_step = 0.25


def stencil(source, axis):
    widened = source.astype(jnp.float32)
    near_diff = jnp.roll(widened, -1, axis) - jnp.roll(widened, 1, axis)
    far_diff = jnp.roll(widened, -2, axis) - jnp.roll(widened, 2, axis)
    return (near_coef * near_diff + far_coef * far_diff).astype(jnp.bfloat16)


def stream_derivative(pencil, stream_inverse):
    right_side = stencil(pencil, 1)
    product = jnp.einsum(
        "ij,kjp->kip", stream_inverse, right_side, preferred_element_type=jnp.float32
    )
    return product.astype(jnp.bfloat16)


def span_derivative(pencil, span_inverse):
    right_side = stencil(pencil, 2)
    product = jnp.einsum(
        "ij,kajy->kaiy", span_inverse, right_side, preferred_element_type=jnp.float32
    )
    return product.astype(jnp.bfloat16)


def wall_derivative(source, wall_operator, metric):
    product = jnp.einsum("kxzj,ij->kxzi", source, wall_operator, preferred_element_type=jnp.float32)
    return product * metric


def span_apply(source, span_inverse):
    derived = span_derivative(
        lax.all_to_all(source, "gz", split_axis=1, concat_axis=2, tiled=True), span_inverse
    )
    return lax.all_to_all(derived, "gz", split_axis=2, concat_axis=1, tiled=True)


def on_device(adjoint, strain, correction, metric, stream_inverse, span_inverse, wall_operator):
    components, stream_cells, span_cells, wall_cells = adjoint.shape
    strain_wide = strain.astype(jnp.float32)
    viscosity = (correction[None] * strain_wide).astype(jnp.bfloat16)
    viscous = viscosity.astype(jnp.float32)[None]
    joined = jnp.concatenate([adjoint, viscosity[None]], 0)
    joined = joined.reshape(components + 1, stream_cells, span_cells * wall_cells)
    pencil = lax.all_to_all(joined, "gx", split_axis=2, concat_axis=1, tiled=True)
    stream_grad = stream_derivative(pencil[:components], stream_inverse)
    pencil_flux = pencil[components:].astype(jnp.float32) * stream_grad.astype(jnp.float32)
    stream_flux = pencil_flux.astype(jnp.bfloat16)
    stream_diverge = stream_derivative(stream_flux, stream_inverse)
    returned = lax.all_to_all(
        jnp.concatenate([stream_grad, stream_diverge], 0),
        "gx",
        split_axis=1,
        concat_axis=2,
        tiled=True,
    )
    returned = returned.reshape(2 * components, stream_cells, span_cells, wall_cells)
    stream_grad = returned[:components]
    stream_diverge = returned[components:]
    span_grad = span_apply(adjoint, span_inverse)
    span_flux = (viscous * span_grad.astype(jnp.float32)).astype(jnp.bfloat16)
    span_diverge = span_apply(span_flux, span_inverse)
    wall_grad = wall_derivative(adjoint, wall_operator, metric).astype(jnp.bfloat16)
    wall_flux = (viscous * wall_grad.astype(jnp.float32)).astype(jnp.bfloat16)
    wall_diverge = wall_derivative(wall_flux, wall_operator, metric)
    total = stream_diverge.astype(jnp.float32) + wall_diverge + span_diverge.astype(jnp.float32)
    updated = (adjoint.astype(jnp.float32) + time_step * total).astype(jnp.bfloat16)
    squares = stream_grad.astype(jnp.float32) ** 2 + wall_grad.astype(jnp.float32) ** 2
    squares = jnp.sum(squares + span_grad.astype(jnp.float32) ** 2, axis=0)
    partial_sum = jnp.sum(strain_wide * squares, axis=0)
    summed = lax.psum_scatter(partial_sum, "gx", scatter_dimension=1, tiled=True)
    gradient = -summed / (stream_cells * lax.axis_size("gx"))
    return (updated, gradient)


MESH = pl.DeviceIdType.MESH
F32 = jnp.float32
BF16 = jnp.bfloat16


def positions(rows, columns):
    return (
        lax.broadcasted_iota(jnp.int32, (rows, columns), 0),
        lax.broadcasted_iota(jnp.int32, (rows, columns), 1),
    )


def as_matrix(condition):
    return jnp.where(condition, 1.0, 0.0).astype(BF16)


def matmul(left, right):
    return jnp.dot(left, right, preferred_element_type=F32)


def matmul_transposed(left, right):
    return lax.dot_general(left, right, (((1,), (1,)), ((), ())), preferred_element_type=F32)


def folded(inverse):
    wide = inverse.astype(F32)
    order = wide.shape[1]
    row, column = positions(order, order)
    gap = lax.rem(row - column + order, order)
    near = as_matrix(gap == order - 1).astype(F32) - as_matrix(gap == 1).astype(F32)
    far = as_matrix(gap == order - 2).astype(F32) - as_matrix(gap == 2).astype(F32)
    both = near_coef * matmul(inverse, near.astype(BF16)) + far_coef * matmul(
        inverse, far.astype(BF16)
    )
    return both.astype(BF16)


def kernel(
    n,
    adjoint,
    strain,
    correction,
    metric,
    stream_inverse,
    span_inverse,
    wall_operator,
    updated,
    gradient,
    out_x,
    got_x,
    back_x,
    home_x,
    span,
    span_matrix,
    span_held,
    total,
    parts_out,
    parts_in,
    x_send,
    x_recv,
    b_send,
    b_recv,
    z_send,
    z_recv,
    g_send,
    g_recv,
):
    me = lax.axis_index("gx")
    side = lax.axis_index("gz")
    other = 1 - side
    components, cells, spans, walls = adjoint.shape
    rows = cells * spans
    width = spans // n
    block = cells * width
    lines = n * block

    barrier = pltpu.get_barrier_semaphore()

    def greet(step, carry):
        peer = lax.rem(me + step, n)
        pl.semaphore_signal(barrier, inc=1, device_id=(peer, side), device_id_type=MESH)
        return carry

    lax.fori_loop(1, n, greet, 0)
    pl.semaphore_signal(barrier, inc=1, device_id=(me, other), device_id_type=MESH)

    row, column = positions(rows, rows)
    source_row = (
        lax.rem(lax.div(row, width), cells) * spans
        + lax.div(row, block) * width
        + lax.rem(row, width)
    )
    to_blocks = as_matrix(column == source_row)
    source_column = (
        lax.rem(lax.div(column, width), cells) * spans
        + lax.div(column, block) * width
        + lax.rem(column, width)
    )
    from_blocks = as_matrix(row == source_column)

    def blocked(field):
        return matmul(to_blocks, field).astype(BF16).reshape(n, block, walls)

    strain_here = strain[...]
    strain_wide = strain_here.astype(F32)
    viscous = (correction[...][None] * strain_wide).astype(BF16).reshape(rows, walls)
    out_x[0] = blocked(strain_here.reshape(rows, walls))
    out_x[1] = blocked(adjoint[0].reshape(rows, walls))
    span[0, side] = viscous
    for c in range(components):
        span[1 + c, side] = adjoint[c].reshape(rows, walls)

    pl.semaphore_wait(barrier, n)

    def fields_of(chunk):
        return pl.ds(0, 2) if chunk == 0 else pl.ds(chunk + 1, 1)

    def x_copy(chunk, peer, slot):
        fields = fields_of(chunk)
        return pltpu.make_async_remote_copy(
            src_ref=out_x.at[fields, peer],
            dst_ref=got_x.at[fields, slot],
            send_sem=x_send.at[chunk, peer],
            recv_sem=x_recv.at[chunk, slot],
            device_id=(peer, side),
            device_id_type=MESH,
        )

    def b_copy(chunk, peer, slot):
        return pltpu.make_async_remote_copy(
            src_ref=back_x.at[chunk, peer],
            dst_ref=home_x.at[chunk, slot],
            send_sem=b_send.at[chunk, peer],
            recv_sem=b_recv.at[chunk, slot],
            device_id=(peer, side),
            device_id_type=MESH,
        )

    def g_copy(chunk, peer, slot):
        return pltpu.make_async_remote_copy(
            src_ref=parts_out.at[peer],
            dst_ref=parts_in.at[slot],
            send_sem=g_send.at[peer],
            recv_sem=g_recv.at[slot],
            device_id=(peer, side),
            device_id_type=MESH,
        )

    def z_copy(field, half):
        return pltpu.make_async_remote_copy(
            src_ref=span.at[field, half],
            dst_ref=span.at[field, half],
            send_sem=z_send.at[field],
            recv_sem=z_recv.at[field],
            device_id=(me, other),
            device_id_type=MESH,
        )

    def send_all(copy, chunk):
        def one(step, carry):
            peer = lax.rem(me + step, n)
            copy(chunk, peer, me).start()
            return carry

        lax.fori_loop(n // 2, n, one, 0)
        lax.fori_loop(1, n // 2, one, 0)

    def receive_all(copy, chunk):
        def one(step, carry):
            peer = lax.rem(me + step, n)
            copy(chunk, peer, peer).wait_recv()
            return carry

        lax.fori_loop(1, n, one, 0)

    def sent_all(copy, chunk):
        def one(step, carry):
            peer = lax.rem(me + step, n)
            copy(chunk, peer, me).wait_send()
            return carry

        lax.fori_loop(1, n, one, 0)

    send_all(x_copy, 0)
    for field in range(components + 1):
        z_copy(field, side).start()
    for c in range(1, components):
        out_x[1 + c] = blocked(adjoint[c].reshape(rows, walls))
        send_all(x_copy, c)
    for field in range(components + 1):
        got_x[field, me] = out_x[field, me]

    wall = wall_operator[...]
    stretch = metric[...]
    squares = jnp.zeros((rows, walls), F32)
    viscous_wide = viscous.astype(F32)
    for c in range(components):
        field = adjoint[c].reshape(rows, walls)
        slope = (matmul_transposed(field, wall) * stretch).astype(BF16)
        slope_wide = slope.astype(F32)
        flux = (viscous_wide * slope_wide).astype(BF16)
        diverge = matmul_transposed(flux, wall) * stretch
        total[c] = field.astype(F32) + time_step * diverge
        squares = squares + slope_wide * slope_wide
    span_held[0] = squares

    row, column = positions(lines, lines // width)
    spread = as_matrix(lax.div(row, width) == column)
    row, column = positions(lines, lines)
    same = lax.rem(row, width) == lax.rem(column, width)
    stream = matmul_transposed(
        matmul(spread, folded(stream_inverse[...])).astype(BF16), spread
    )
    stream = jnp.where(same, stream, 0.0).astype(BF16)

    row, column = positions(2 * rows, 2 * spans)
    spread = as_matrix(lax.div(row, rows) * spans + lax.rem(row, spans) == column)
    row, column = positions(2 * rows, 2 * rows)
    same = lax.rem(lax.div(row, spans), cells) == lax.rem(lax.div(column, spans), cells)
    both = matmul_transposed(
        matmul(spread, folded(span_inverse[...])).astype(BF16), spread
    )
    both = jnp.where(same, both, 0.0).astype(BF16)
    span_matrix[...] = both.reshape(2, rows, 2 * rows)

    line_row = lax.broadcasted_iota(jnp.int32, (lines, walls), 0)
    owned = jnp.zeros((lines, walls), F32)
    for w in range(width):
        values = correction[pl.ds(me * width + w, 1), :]
        owned = jnp.where(lax.rem(line_row, width) == w, values, owned)

    receive_all(x_copy, 0)
    line_strain = got_x[0].reshape(lines, walls).astype(F32)
    line_viscous = (owned * line_strain).astype(BF16).astype(F32)
    line_squares = jnp.zeros((lines, walls), F32)
    for c in range(components):
        if c > 0:
            receive_all(x_copy, c)
        slope = matmul(stream, got_x[1 + c].reshape(lines, walls)).astype(BF16)
        slope_wide = slope.astype(F32)
        flux = (line_viscous * slope_wide).astype(BF16)
        back_x[c] = matmul(stream, flux).astype(BF16).reshape(n, block, walls)
        send_all(b_copy, c)
        home_x[c, me] = back_x[c, me]
        line_squares = line_squares + slope_wide * slope_wide
    weighted = line_strain * line_squares

    z_copy(0, other).wait_recv()
    viscous_both = span[0].reshape(2 * rows, walls).astype(F32)
    for c in range(components):
        z_copy(1 + c, other).wait_recv()
        slope = matmul(both, span[1 + c].reshape(2 * rows, walls)).astype(BF16)
        slope_wide = slope.astype(F32)
        flux = (viscous_both * slope_wide).astype(BF16)
        diverge = matmul(span_matrix[side], flux).astype(BF16).astype(F32)
        total[c] = total[c] + time_step * diverge
        own = jnp.where(side == 0, slope_wide[:rows], slope_wide[rows:])
        span_held[0] = span_held[0] + own * own

    partial = jnp.sum(strain_wide * span_held[0].reshape(cells, spans, walls), axis=0)
    span_row = lax.broadcasted_iota(jnp.int32, (spans, walls), 0)
    for w in range(width):
        chosen = jnp.where(lax.rem(line_row, width) == w, weighted, 0.0)
        summed = jnp.sum(chosen, axis=0, keepdims=True)
        partial = partial + jnp.where(span_row == me * width + w, summed, 0.0)
    padded = jnp.concatenate([partial, jnp.zeros((128 - spans, walls), F32)], axis=0)
    parts_out[...] = padded.T.reshape(n, walls // n, 128)
    send_all(g_copy, 0)
    parts_in[me] = parts_out[me]

    for c in range(components):
        receive_all(b_copy, c)
        moved = matmul(from_blocks, home_x[c].reshape(lines, walls))
        result = total[c] + time_step * moved
        updated[c] = result.astype(BF16).reshape(cells, spans, walls)

    receive_all(g_copy, 0)
    whole = jnp.sum(parts_in[...], axis=0) * (-1.0 / (cells * n))
    tall = jnp.concatenate([whole, jnp.zeros((128 - walls // n, 128), F32)], axis=0)
    gradient[...] = tall.T[:spans, : walls // n]

    for c in range(components):
        sent_all(x_copy, c)
        sent_all(b_copy, c)
    sent_all(g_copy, 0)
    for field in range(components + 1):
        z_copy(field, side).wait_send()


def in_one_kernel(
    n, adjoint, strain, correction, metric, stream_inverse, span_inverse, wall_operator
):
    components, cells, spans, walls = adjoint.shape
    rows = cells * spans
    block = rows // n
    vmem = pl.BlockSpec(memory_space=pltpu.VMEM)
    blocks = (n, block, walls)
    dma = pltpu.SemaphoreType.DMA
    return tuple(
        pl.pallas_call(
            functools.partial(kernel, n),
            out_shape=(
                jax.ShapeDtypeStruct(adjoint.shape, BF16),
                jax.ShapeDtypeStruct((spans, walls // n), F32),
            ),
            in_specs=[vmem] * 7,
            out_specs=(vmem, vmem),
            scratch_shapes=[
                pltpu.VMEM((components + 1,) + blocks, BF16),
                pltpu.VMEM((components + 1,) + blocks, BF16),
                pltpu.VMEM((components,) + blocks, BF16),
                pltpu.VMEM((components,) + blocks, BF16),
                pltpu.VMEM((components + 1, 2, rows, walls), BF16),
                pltpu.VMEM((2, rows, 2 * rows), BF16),
                pltpu.VMEM((1, rows, walls), F32),
                pltpu.VMEM((components, rows, walls), F32),
                pltpu.VMEM((n, walls // n, 128), F32),
                pltpu.VMEM((n, walls // n, 128), F32),
                dma((components, n)),
                dma((components, n)),
                dma((components, n)),
                dma((components, n)),
                dma((components + 1,)),
                dma((components + 1,)),
                dma((n,)),
                dma((n,)),
            ],
            compiler_params=pltpu.CompilerParams(
                collective_id=0, has_side_effects=True, vmem_limit_bytes=40 * 1024 * 1024
            ),
        )(
            adjoint,
            strain,
            correction,
            metric.reshape(1, walls),
            stream_inverse,
            span_inverse,
            wall_operator,
        )
    )


def on_each(mesh, adjoint, strain, *rest):
    n = mesh.shape["gx"]
    _, cells, spans, walls = adjoint.shape
    small = mesh.shape["gz"] == 2 and spans % n == 0 and spans <= 128
    if small and cells * spans // n % 16 == 0 and walls // n % 8 == 0 and walls // n <= 128:
        return in_one_kernel(n, adjoint, strain, *rest)
    return on_device(adjoint, strain, *rest)


def solution(mesh):
    in_specs = (P(None, "gx", "gz", None), P("gx", "gz", None), P("gz", None), P(), P(), P(), P())
    out_specs = (P(None, "gx", "gz", None), P("gz", "gx"))
    return jax.shard_map(
        functools.partial(on_each, mesh),
        mesh=mesh,
        in_specs=in_specs,
        out_specs=out_specs,
        check_vma=False,
    )
```

```python
import functools

import jax
import jax.numpy as jnp
from jax import lax
from jax.experimental import pallas as pl
from jax.experimental.pallas import tpu as pltpu
from jax.sharding import PartitionSpec as P

near_coef = 7.0 / 9.0
far_coef = 1.0 / 36.0
time_step = 0.25


def stencil(source, axis):
    widened = source.astype(jnp.float32)
    near_diff = jnp.roll(widened, -1, axis) - jnp.roll(widened, 1, axis)
    far_diff = jnp.roll(widened, -2, axis) - jnp.roll(widened, 2, axis)
    return (near_coef * near_diff + far_coef * far_diff).astype(jnp.bfloat16)


def stream_derivative(pencil, stream_inverse):
    right_side = stencil(pencil, 1)
    product = jnp.einsum(
        "ij,kjp->kip", stream_inverse, right_side, preferred_element_type=jnp.float32
    )
    return product.astype(jnp.bfloat16)


def span_derivative(pencil, span_inverse):
    right_side = stencil(pencil, 2)
    product = jnp.einsum(
        "ij,kajy->kaiy", span_inverse, right_side, preferred_element_type=jnp.float32
    )
    return product.astype(jnp.bfloat16)


def wall_derivative(source, wall_operator, metric):
    product = jnp.einsum("kxzj,ij->kxzi", source, wall_operator, preferred_element_type=jnp.float32)
    return product * metric


def span_apply(source, span_inverse):
    derived = span_derivative(
        lax.all_to_all(source, "gz", split_axis=1, concat_axis=2, tiled=True), span_inverse
    )
    return lax.all_to_all(derived, "gz", split_axis=2, concat_axis=1, tiled=True)


def on_device(adjoint, strain, correction, metric, stream_inverse, span_inverse, wall_operator):
    components, stream_cells, span_cells, wall_cells = adjoint.shape
    strain_wide = strain.astype(jnp.float32)
    viscosity = (correction[None] * strain_wide).astype(jnp.bfloat16)
    viscous = viscosity.astype(jnp.float32)[None]
    joined = jnp.concatenate([adjoint, viscosity[None]], 0)
    joined = joined.reshape(components + 1, stream_cells, span_cells * wall_cells)
    pencil = lax.all_to_all(joined, "gx", split_axis=2, concat_axis=1, tiled=True)
    stream_grad = stream_derivative(pencil[:components], stream_inverse)
    pencil_flux = pencil[components:].astype(jnp.float32) * stream_grad.astype(jnp.float32)
    stream_flux = pencil_flux.astype(jnp.bfloat16)
    stream_diverge = stream_derivative(stream_flux, stream_inverse)
    returned = lax.all_to_all(
        jnp.concatenate([stream_grad, stream_diverge], 0),
        "gx",
        split_axis=1,
        concat_axis=2,
        tiled=True,
    )
    returned = returned.reshape(2 * components, stream_cells, span_cells, wall_cells)
    stream_grad = returned[:components]
    stream_diverge = returned[components:]
    span_grad = span_apply(adjoint, span_inverse)
    span_flux = (viscous * span_grad.astype(jnp.float32)).astype(jnp.bfloat16)
    span_diverge = span_apply(span_flux, span_inverse)
    wall_grad = wall_derivative(adjoint, wall_operator, metric).astype(jnp.bfloat16)
    wall_flux = (viscous * wall_grad.astype(jnp.float32)).astype(jnp.bfloat16)
    wall_diverge = wall_derivative(wall_flux, wall_operator, metric)
    total = stream_diverge.astype(jnp.float32) + wall_diverge + span_diverge.astype(jnp.float32)
    updated = (adjoint.astype(jnp.float32) + time_step * total).astype(jnp.bfloat16)
    squares = stream_grad.astype(jnp.float32) ** 2 + wall_grad.astype(jnp.float32) ** 2
    squares = jnp.sum(squares + span_grad.astype(jnp.float32) ** 2, axis=0)
    partial_sum = jnp.sum(strain_wide * squares, axis=0)
    summed = lax.psum_scatter(partial_sum, "gx", scatter_dimension=1, tiled=True)
    gradient = -summed / (stream_cells * lax.axis_size("gx"))
    return (updated, gradient)


MESH = pl.DeviceIdType.MESH
field_chunks = ((0, 2), (2, 1), (3, 1))
back_chunks = ((0, 1), (1, 1), (2, 1))
F32 = jnp.float32
BF16 = jnp.bfloat16


def positions(rows, columns):
    return (
        lax.broadcasted_iota(jnp.int32, (rows, columns), 0),
        lax.broadcasted_iota(jnp.int32, (rows, columns), 1),
    )


def as_matrix(condition):
    return jnp.where(condition, 1.0, 0.0).astype(BF16)


def matmul(left, right):
    return jnp.dot(left, right, preferred_element_type=F32)


def matmul_transposed(left, right):
    return lax.dot_general(left, right, (((1,), (1,)), ((), ())), preferred_element_type=F32)


def folded(inverse):
    wide = inverse.astype(F32)
    order = wide.shape[1]
    row, column = positions(order, order)
    gap = lax.rem(row - column + order, order)
    near = as_matrix(gap == order - 1).astype(F32) - as_matrix(gap == 1).astype(F32)
    far = as_matrix(gap == order - 2).astype(F32) - as_matrix(gap == 2).astype(F32)
    both = near_coef * matmul(inverse, near.astype(BF16)) + far_coef * matmul(
        inverse, far.astype(BF16)
    )
    return both.astype(BF16)


def kernel(
    n,
    cells,
    adjoint,
    strain_far,
    correction_far,
    metric_far,
    stream_far,
    span_far,
    wall_far,
    updated_far,
    gradient_far,
    updated,
    gradient,
    stored,
    strain,
    correction,
    metric,
    stream_inverse,
    span_inverse,
    wall_operator,
    loaded,
    out_x,
    got_x,
    back_x,
    home_x,
    span,
    span_matrix,
    span_held,
    total,
    parts_out,
    parts_in,
    tall,
    short,
    x_send,
    x_recv,
    b_send,
    b_recv,
    z_send,
    z_recv,
    g_send,
    g_recv,
):
    me = lax.axis_index("gx")
    side = lax.axis_index("gz")
    other = 1 - side
    components, rows, walls = adjoint.shape
    spans = rows // cells
    width = spans // n
    block = cells * width
    lines = n * block

    barrier = pltpu.get_barrier_semaphore()

    def greet(step, carry):
        peer = lax.rem(me + step, n)
        pl.semaphore_signal(barrier, inc=1, device_id=(peer, side), device_id_type=MESH)
        return carry

    lax.fori_loop(1, n, greet, 0)
    pl.semaphore_signal(barrier, inc=1, device_id=(me, other), device_id_type=MESH)

    loads = [(strain_far, strain), (adjoint.at[0], span.at[1, side]), (correction_far, correction)]
    loads += [(adjoint.at[c], span.at[1 + c, side]) for c in range(1, components)]
    loads += [(wall_far, wall_operator), (metric_far, metric)]
    loads += [(stream_far, stream_inverse), (span_far, span_inverse)]
    loads = [
        pltpu.make_async_copy(source, target, loaded.at[k])
        for k, (source, target) in enumerate(loads)
    ]
    for load in loads:
        load.start()

    row, column = positions(rows, rows)
    source_row = (
        lax.rem(lax.div(row, width), cells) * spans
        + lax.div(row, block) * width
        + lax.rem(row, width)
    )
    to_blocks = as_matrix(column == source_row)
    source_column = (
        lax.rem(lax.div(column, width), cells) * spans
        + lax.div(column, block) * width
        + lax.rem(column, width)
    )
    from_blocks = as_matrix(row == source_column)

    def blocked(field):
        return matmul(to_blocks, field).astype(BF16).reshape(n, block, walls)

    for load in loads[:2]:
        load.wait()
    out_x[:, 0] = blocked(strain[...])
    out_x[:, 1] = blocked(span[1, side])
    for load in loads[2:]:
        load.wait()
    strain_wide = strain[...].astype(F32).reshape(cells, spans, walls)
    viscous = (correction[...][None] * strain_wide).astype(BF16).reshape(rows, walls)
    span[0, side] = viscous

    pl.semaphore_wait(barrier, n)

    def x_copy(chunk, peer, slot):
        fields = pl.ds(*field_chunks[chunk])
        return pltpu.make_async_remote_copy(
            src_ref=out_x.at[peer, fields],
            dst_ref=got_x.at[slot, fields],
            send_sem=x_send.at[chunk, peer],
            recv_sem=x_recv.at[chunk, slot],
            device_id=(peer, side),
            device_id_type=MESH,
        )

    def b_copy(chunk, peer, slot):
        fields = pl.ds(*back_chunks[chunk])
        return pltpu.make_async_remote_copy(
            src_ref=back_x.at[peer, fields],
            dst_ref=home_x.at[slot, fields],
            send_sem=b_send.at[chunk, peer],
            recv_sem=b_recv.at[chunk, slot],
            device_id=(peer, side),
            device_id_type=MESH,
        )

    def g_copy(chunk, peer, slot):
        return pltpu.make_async_remote_copy(
            src_ref=parts_out.at[peer],
            dst_ref=parts_in.at[slot],
            send_sem=g_send.at[peer],
            recv_sem=g_recv.at[slot],
            device_id=(peer, side),
            device_id_type=MESH,
        )

    def z_copy(field, half):
        return pltpu.make_async_remote_copy(
            src_ref=span.at[field, half],
            dst_ref=span.at[field, half],
            send_sem=z_send.at[field],
            recv_sem=z_recv.at[field],
            device_id=(me, other),
            device_id_type=MESH,
        )

    def send_all(copy, chunk):
        def one(step, carry):
            peer = lax.rem(me + step, n)
            copy(chunk, peer, me).start()
            return carry

        lax.fori_loop(n // 2, n, one, 0)
        lax.fori_loop(1, n // 2, one, 0)

    def receive_all(copy, chunk):
        def one(step, carry):
            peer = lax.rem(me + step, n)
            copy(chunk, peer, peer).wait_recv()
            return carry

        lax.fori_loop(1, n, one, 0)

    def sent_all(copy, chunk):
        def one(step, carry):
            peer = lax.rem(me + step, n)
            copy(chunk, peer, me).wait_send()
            return carry

        lax.fori_loop(1, n, one, 0)

    send_all(x_copy, 0)
    for field in range(components + 1):
        z_copy(field, side).start()
    for chunk, (start, count) in enumerate(field_chunks[1:], 1):
        for field in range(start, start + count):
            out_x[:, field] = blocked(span[field, side])
        send_all(x_copy, chunk)
    got_x[me] = out_x[me]

    wall = wall_operator[...]
    stretch = metric[...]
    squares = jnp.zeros((rows, walls), F32)
    viscous_wide = viscous.astype(F32)
    for c in range(components):
        field = span[1 + c, side]
        slope = (matmul_transposed(field, wall) * stretch).astype(BF16)
        slope_wide = slope.astype(F32)
        flux = (viscous_wide * slope_wide).astype(BF16)
        diverge = matmul_transposed(flux, wall) * stretch
        total[c] = field.astype(F32) + time_step * diverge
        squares = squares + slope_wide * slope_wide
    span_held[0] = squares

    row, column = positions(lines, lines // width)
    spread = as_matrix(lax.div(row, width) == column)
    row, column = positions(lines, lines)
    same = lax.rem(row, width) == lax.rem(column, width)
    stream = matmul_transposed(
        matmul(spread, folded(stream_inverse[...])).astype(BF16), spread
    )
    stream = jnp.where(same, stream, 0.0).astype(BF16)

    row, column = positions(2 * rows, 2 * spans)
    spread = as_matrix(lax.div(row, rows) * spans + lax.rem(row, spans) == column)
    row, column = positions(2 * rows, 2 * rows)
    same = lax.rem(lax.div(row, spans), cells) == lax.rem(lax.div(column, spans), cells)
    both = matmul_transposed(
        matmul(spread, folded(span_inverse[...])).astype(BF16), spread
    )
    both = jnp.where(same, both, 0.0).astype(BF16)
    span_matrix[...] = both.reshape(2, rows, 2 * rows)

    line_row = lax.broadcasted_iota(jnp.int32, (lines, walls), 0)
    owned = jnp.zeros((lines, walls), F32)
    for w in range(width):
        values = correction[pl.ds(me * width + w, 1), :]
        owned = jnp.where(lax.rem(line_row, width) == w, values, owned)

    line_squares = jnp.zeros((lines, walls), F32)
    for chunk, (start, count) in enumerate(back_chunks):
        receive_all(x_copy, chunk)
        if chunk == 0:
            line_strain = got_x[:, 0].reshape(lines, walls).astype(F32)
            line_viscous = (owned * line_strain).astype(BF16).astype(F32)
        for c in range(start, start + count):
            slope = matmul(stream, got_x[:, 1 + c].reshape(lines, walls)).astype(BF16)
            slope_wide = slope.astype(F32)
            flux = (line_viscous * slope_wide).astype(BF16)
            back_x[:, c] = matmul(stream, flux).astype(BF16).reshape(n, block, walls)
            line_squares = line_squares + slope_wide * slope_wide
        send_all(b_copy, chunk)
    home_x[me] = back_x[me]
    weighted = line_strain * line_squares

    z_copy(0, other).wait_recv()
    viscous_both = span[0].reshape(2 * rows, walls).astype(F32)
    for c in range(components):
        z_copy(1 + c, other).wait_recv()
        slope = matmul(both, span[1 + c].reshape(2 * rows, walls)).astype(BF16)
        slope_wide = slope.astype(F32)
        flux = (viscous_both * slope_wide).astype(BF16)
        diverge = matmul(span_matrix[side], flux).astype(BF16).astype(F32)
        total[c] = total[c] + time_step * diverge
        own = jnp.where(side == 0, slope_wide[:rows], slope_wide[rows:])
        span_held[0] = span_held[0] + own * own

    partial = jnp.sum(strain_wide * span_held[0].reshape(cells, spans, walls), axis=0)
    span_row = lax.broadcasted_iota(jnp.int32, (spans, walls), 0)
    for w in range(width):
        chosen = jnp.where(lax.rem(line_row, width) == w, weighted, 0.0)
        summed = jnp.sum(chosen, axis=0, keepdims=True)
        partial = partial + jnp.where(span_row == me * width + w, summed, 0.0)
    padded = jnp.concatenate([partial, jnp.zeros((128 - spans, walls), F32)], axis=0)
    tall[...] = padded.T
    pack = 128 // spans
    deep = walls // (n * pack)
    packed = tall[pl.ds(0, n * deep, stride=pack), :]
    for w in range(1, pack):
        piece = tall[pl.ds(w, n * deep, stride=pack), :]
        packed = packed + pltpu.roll(piece, w * spans, 1)
    for peer in range(n):
        parts_out[peer] = packed[peer * deep : (peer + 1) * deep]
    send_all(g_copy, 0)
    parts_in[me] = parts_out[me]

    stores = [
        pltpu.make_async_copy(updated.at[c], updated_far.at[c], stored.at[c])
        for c in range(components)
    ]
    stores.append(pltpu.make_async_copy(gradient, gradient_far, stored.at[components]))
    for chunk, (start, count) in enumerate(back_chunks):
        receive_all(b_copy, chunk)
        for c in range(start, start + count):
            moved = matmul(from_blocks, home_x[:, c].reshape(lines, walls))
            result = total[c] + time_step * moved
            updated[c] = result.astype(BF16)
            stores[c].start()

    receive_all(g_copy, 0)
    whole = jnp.sum(parts_in[...], axis=0) * (-1.0 / (cells * n))
    for w in range(pack):
        piece = whole if w == 0 else pltpu.roll(whole, 128 - w * spans, 1)
        short[pl.ds(w, deep, stride=pack), :] = piece
    gradient[...] = short[:, :spans]
    stores[components].start()

    for chunk in range(len(back_chunks)):
        sent_all(x_copy, chunk)
        sent_all(b_copy, chunk)
    sent_all(g_copy, 0)
    for field in range(components + 1):
        z_copy(field, side).wait_send()
    for store in stores:
        store.wait()


def in_one_kernel(
    n, adjoint, strain, correction, metric, stream_inverse, span_inverse, wall_operator
):
    components, cells, spans, walls = adjoint.shape
    rows = cells * spans
    vmem = pl.BlockSpec(memory_space=pltpu.VMEM)
    far = pl.BlockSpec(memory_space=pltpu.HBM)
    block = (rows // n, walls)
    deep = walls // n * spans // 128
    dma = pltpu.SemaphoreType.DMA
    updated, gradient = pl.pallas_call(
        functools.partial(kernel, n, cells),
        out_shape=(
            jax.ShapeDtypeStruct((components, rows, walls), BF16),
            jax.ShapeDtypeStruct((walls // n, spans), F32),
        ),
        in_specs=[far] * 7,
        out_specs=(far, far),
        scratch_shapes=[
            pltpu.VMEM((components, rows, walls), BF16),
            pltpu.VMEM((walls // n, spans), F32),
            dma((components + 1,)),
            pltpu.VMEM((rows, walls), BF16),
            pltpu.VMEM(correction.shape, F32),
            pltpu.VMEM((1, walls), F32),
            pltpu.VMEM(stream_inverse.shape, BF16),
            pltpu.VMEM(span_inverse.shape, BF16),
            pltpu.VMEM(wall_operator.shape, BF16),
            dma((components + 6,)),
            pltpu.VMEM((n, components + 1) + block, BF16),
            pltpu.VMEM((n, components + 1) + block, BF16),
            pltpu.VMEM((n, components) + block, BF16),
            pltpu.VMEM((n, components) + block, BF16),
            pltpu.VMEM((components + 1, 2, rows, walls), BF16),
            pltpu.VMEM((2, rows, 2 * rows), BF16),
            pltpu.VMEM((1, rows, walls), F32),
            pltpu.VMEM((components, rows, walls), F32),
            pltpu.VMEM((n, deep, 128), F32),
            pltpu.VMEM((n, deep, 128), F32),
            pltpu.VMEM((walls, 128), F32),
            pltpu.VMEM((walls // n, 128), F32),
            dma((components, n)),
            dma((components, n)),
            dma((components, n)),
            dma((components, n)),
            dma((components + 1,)),
            dma((components + 1,)),
            dma((n,)),
            dma((n,)),
        ],
        compiler_params=pltpu.CompilerParams(
            collective_id=0, has_side_effects=True, vmem_limit_bytes=64 * 1024 * 1024 - 65536
        ),
    )(
        adjoint.reshape(components, rows, walls),
        strain.reshape(rows, walls),
        correction,
        metric.reshape(1, walls),
        stream_inverse,
        span_inverse,
        wall_operator,
    )
    return updated.reshape(adjoint.shape), gradient.T


def on_each(mesh, adjoint, strain, *rest):
    n = mesh.shape["gx"]
    _, cells, spans, walls = adjoint.shape
    small = len(adjoint) == 3 and walls // n * spans % 128 == 0 and 128 % spans == 0 and walls // n * spans >= 128
    small = small and mesh.shape["gz"] == 2 and spans % n == 0 and spans <= 128
    if small and cells * spans // n % 16 == 0 and walls // n % 8 == 0 and walls // n <= 128:
        return in_one_kernel(n, adjoint, strain, *rest)
    return on_device(adjoint, strain, *rest)


def solution(mesh):
    in_specs = (P(None, "gx", "gz", None), P("gx", "gz", None), P("gz", None), P(), P(), P(), P())
    out_specs = (P(None, "gx", "gz", None), P("gz", "gx"))
    return jax.shard_map(
        functools.partial(on_each, mesh),
        mesh=mesh,
        in_specs=in_specs,
        out_specs=out_specs,
        check_vma=False,
    )
```
